32 devices in a mesh: row: 4 (over z), col: 8 (over y, x, core).
Axes of the slice: x: 2, y: 2, z: 4, core: 2. Of those that a mesh axis runs over, the one named last changes fastest.
Arguments:
- slots: bfloat16 [192, 128, 128], P(('row', 'col')), may hold values from -6 to 6
- block_list: int32 [192], P(('row', 'col')), may hold values from -1 to 63, as said below
- metric: bfloat16 [8192, 1024], P('row', 'col'), may hold values from -0.125 to 0.125
Outputs:
- contracted: float32 [4096, 1024], P('row', 'col')
The draws below stay inside these ranges and needn't reach their ends.
Inputs may be any that keep to these rules, and one draw needn't show every extreme that they name: `block_list`: the live entries of one device's 6 slots come first and name distinct blocks; -1 marks an unused slot; every device has at least 3 live slots and some device has all 6 live.
All inputs are finite; a program needn't handle non-finite values.
Results may differ from the reference program's by a relative error of at most 0.0003.
Values may be sent and summed in bfloat16 or wider, within the bound.
A program may use at most 128 MiB of HBM per device.

```python
import jax
import jax.numpy as jnp
from jax import lax

BLK = 128
PAIR_DEV = 1024
KMAX = 6
NP = 8192
NPAIR = 4096
NQ = 1024
N_ROW = 4
N_COL = 8


def draw_block_list(key, part):
    device_count = N_ROW * N_COL
    tile_blocks = PAIR_DEV // BLK * (NP // N_COL // BLK)
    first_key = jax.random.fold_in(key, 11)
    second_key = jax.random.fold_in(key, 23)
    third_key = jax.random.fold_in(key, 37)
    scores = jax.random.randint(first_key, (device_count, tile_blocks), 0, 1 << 20) * tile_blocks
    scores = scores + jnp.arange(tile_blocks, dtype=jnp.int32)[None, :]
    picked = jnp.argsort(scores, axis=1)[:, :KMAX].astype(jnp.int32)
    counts = jax.random.randint(second_key, (device_count,), (KMAX + 1) // 2, KMAX + 1)
    forced = jax.random.randint(third_key, (), 0, device_count)
    counts = jnp.where(jnp.arange(device_count) == forced, KMAX, counts)
    is_live = jnp.arange(KMAX)[None, :] < counts[:, None]
    return jnp.where(is_live, picked, -1).astype(jnp.int32).reshape(-1)


def levels(own_key, shape, shards, least, top_value):
    factor_of, own = 1.0, jax.random.fold_in(own_key, 6)
    for axis_at, shards_of in shards:
        steps = jnp.exp(jax.random.uniform(jax.random.fold_in(own, axis_at), (shards_of,), jnp.float32, least / len(shards), top_value / len(shards)))
        factor_of = factor_of * jnp.repeat(steps, shape[axis_at] // shards_of).reshape([-1 if axis == axis_at else 1 for axis in range(len(shape))])
    return factor_of


def normal_values(stream_key, dims, width, limit, split=(), held_as=jnp.bfloat16):
    values = width * jax.random.normal(stream_key, dims, jnp.float32)
    if split:
        values = values * levels(stream_key, dims, split, -0.22, 0.18)
    return jnp.clip(values, -limit, limit).astype(held_as)


def setup_inputs(seed: int = 0) -> dict:
    arg_keys = jax.random.split(jax.random.key(seed), 4)
    slots = normal_values(arg_keys[0], (N_ROW * N_COL * KMAX, BLK, BLK), 1.0, 6.0, ((0, 32),))
    block_list = draw_block_list(jax.random.fold_in(arg_keys[3], 71), 0)
    metric = normal_values(arg_keys[2], (NP, NQ), (NP // 4) ** -0.5, 0.125, ((0, 4), (1, 8)))
    return {"slots": slots, "block_list": block_list, "metric": metric}


def reference(slots, block_list, metric):
    pair_blocks = PAIR_DEV // BLK
    col_blocks = NP // N_COL // BLK
    slot_grid = slots.reshape(N_ROW, N_COL * KMAX, BLK, BLK)
    list_grid = block_list.reshape(N_ROW, N_COL * KMAX)
    metric_blocks = metric.reshape(NP // BLK, BLK, NQ)
    shard_of = (jnp.arange(N_COL * KMAX) // KMAX).astype(jnp.int32)

    def one_band(inputs):
        band_slots, band_list = inputs
        clipped = jnp.maximum(band_list, 0)
        is_live = band_list >= 0
        global_block = (shard_of * col_blocks + clipped % col_blocks).astype(jnp.int32)
        pair_block = (clipped // col_blocks).astype(jnp.int32)

        def add_slot(total, entry):
            block, glob, pairb, alive = entry
            rows = metric_blocks[glob]
            prod = jnp.dot(block, rows, preferred_element_type=jnp.float32)
            prod = jnp.where(alive, prod, jnp.zeros_like(prod))
            begin = (pairb * BLK).astype(jnp.int32)
            current = lax.dynamic_slice_in_dim(total, begin, BLK, 0)
            total = lax.dynamic_update_slice_in_dim(total, current + prod, begin, 0)
            return total, None

        start_total = jnp.zeros((PAIR_DEV, NQ), jnp.float32)
        total, _ = lax.scan(add_slot, start_total, (band_slots, global_block, pair_block, is_live))
        return total

    bands = lax.map(one_band, (slot_grid, list_grid))
    return bands.reshape(NPAIR, NQ)
```

```python
import jax
import jax.numpy as jnp
from jax import lax
from jax.experimental import pallas as pl
from jax.experimental.pallas import tpu as pltpu
from jax.sharding import PartitionSpec as P

PAIR_DEV = 1024
MESH = pl.DeviceIdType.MESH


def kernel(n_row, n_col, list_ref, slots_ref, metric_ref, out_ref, own, held, slots, own_list, lists, table, prev, prod, sems):
    row, col = lax.axis_index("row"), lax.axis_index("col")
    number = list_ref.shape[0]
    halves = len(own)
    col_blocks, width = own[0].shape[0], own[0].shape[1]
    pair_blocks = out_ref.shape[0] // width
    zero = n_col * number

    def has(side, d):
        return row + d < n_row if side == 0 else row - d >= 0

    def toward(side):
        return row - 1 if side == 0 else row + 1

    def peer(d):
        return lax.rem(col + d, n_col)

    barrier = pltpu.get_barrier_semaphore()
    for d in range(1, n_col):
        pl.semaphore_signal(barrier, inc=1, device_id=(row, peer(d)), device_id_type=MESH)
    for side in range(2):

        @pl.when(has(side, 1))
        def _():
            pl.semaphore_signal(barrier, inc=1, device_id=(toward(1 - side), col), device_id_type=MESH)

    lane = lax.broadcasted_iota(jnp.int32, own_list.shape, 1)
    tile = jnp.full(own_list.shape, -1, jnp.int32)
    for s in range(number):
        tile = jnp.where(lane == s, list_ref[s], tile)
    own_list[...] = tile
    prod[zero] = jnp.zeros(prod.shape[1:], prod.dtype)

    near = has(0, 1).astype(jnp.int32) + has(1, 1).astype(jnp.int32)
    pl.semaphore_wait(barrier, n_col - 1 + near)

    def list_copy(d):
        return pltpu.make_async_remote_copy(
            src_ref=own_list, dst_ref=lists.at[col], send_sem=sems["list_send"].at[d], recv_sem=sems["list_recv"].at[d],
            device_id=(row, peer(d)), device_id_type=MESH,
        )

    def slot_copy(d):
        return pltpu.make_async_remote_copy(
            src_ref=slots_ref, dst_ref=slots.at[col], send_sem=sems["slot_send"].at[d], recv_sem=sems["slot_recv"].at[d],
            device_id=(row, peer(d)), device_id_type=MESH,
        )

    def metric_copy(side, d, h):
        source = metric_ref.at[pl.ds(h * col_blocks, col_blocks)] if d == 0 else held[side][d - 1][h]
        return pltpu.make_async_remote_copy(
            src_ref=source, dst_ref=held[side][d][h],
            send_sem=sems["metric_send"].at[side, d, h], recv_sem=sems["metric_recv"].at[side, d, h],
            device_id=(toward(side), col), device_id_type=MESH,
        )

    def own_copy(h):
        return pltpu.make_async_copy(metric_ref.at[pl.ds(h * col_blocks, col_blocks)], own[h], sems["own"].at[h])

    own_slots = pltpu.make_async_copy(slots_ref, slots.at[col], sems["slot_recv"].at[0])
    for d in range(1, n_col):
        list_copy(d).start()
    for h in range(halves):
        for side in range(2):

            @pl.when(has(1 - side, 1))
            def _():
                metric_copy(side, 0, h).start()

    for d in range(1, n_col):
        slot_copy(d).start()
    own_slots.start()
    for h in range(halves):
        own_copy(h).start()

    lists[col] = own_list[...]
    for d in range(1, n_col):
        list_copy(d).wait_recv()
    to_scalars = pltpu.make_async_copy(lists, table, sems["table"].at[0])
    to_scalars.start()
    to_scalars.wait()

    steps = [(0, 0)] + [(side, d) for d in range(1, n_row) for side in range(2)]
    last = [jnp.int32(zero)] * pair_blocks
    for at, (side, d) in enumerate(steps):
        shard = row + d if side == 0 else row - d
        valid = has(side, d)
        shard = jnp.clip(shard, 0, n_row - 1)
        for h in range(halves):
            group = shard * halves + h
            for s in range(number):
                v = table[group, 0, s]
                pair = jnp.where(jnp.logical_and(valid, v >= 0), lax.div(jnp.maximum(v, 0), jnp.int32(col_blocks)), -1)
                before = jnp.int32(zero)
                here = group * number + s
                for p in range(pair_blocks):
                    before = jnp.where(pair == p, last[p], before)
                    last[p] = jnp.where(pair == p, here, last[p])
                prev[(at * halves + h) * number + s] = before

    def forward(d):
        for h in range(halves):
            for side in range(2):

                @pl.when(has(side, d))
                def _():
                    metric_copy(side, d - 1, h).wait_recv()
                    if d < n_row - 1:

                        @pl.when(has(1 - side, 1))
                        def _():
                            metric_copy(side, d, h).start()

    def compute(at):
        side, d = steps[at]
        shard = row + d if side == 0 else row - d

        @pl.when(has(side, d))
        def _():
            for h in range(halves):
                group = shard * halves + h
                rows = own[h] if d == 0 else held[side][d - 1][h]
                if d == 0:
                    own_copy(h).wait()
                arrived = sems["slot_recv"].at[lax.rem(col - group + n_col, n_col)]
                pltpu.make_async_copy(slots_ref, slots.at[group], arrived).wait()
                for s in range(number):
                    v = jnp.maximum(table[group, 0, s], 0)
                    before = prev[(at * halves + h) * number + s]
                    block = rows[lax.rem(v, jnp.int32(col_blocks))]
                    product = jnp.dot(slots[group, s], block, preferred_element_type=jnp.float32)
                    prod[group * number + s] = prod[before] + product

    forward(1)
    compute(0)
    for d in range(1, n_row):
        if d < n_row - 1:
            forward(d + 1)
        compute(2 * d - 1)
        compute(2 * d)

    for p in range(pair_blocks):
        out_ref[pl.ds(p * width, width)] = prod[last[p]]

    for d in range(1, n_col):
        list_copy(d).wait_send()
        slot_copy(d).wait_send()
    for d in range(n_row - 1):
        for h in range(halves):
            for side in range(2):

                @pl.when(jnp.logical_and(has(side, d), has(1 - side, 1)))
                def _():
                    metric_copy(side, d, h).wait_send()


def on_device(slots, block_list, metric):
    n_row, n_col = lax.axis_size("row"), lax.axis_size("col")
    number, width = slots.shape[:2]
    out_cols = metric.shape[1]
    halves = n_col // n_row
    shard_blocks = metric.shape[0] // width
    col_blocks = shard_blocks // halves
    half = pltpu.VMEM((col_blocks, width, out_cols), metric.dtype)
    groups = 2 * n_row - 1
    dma = pltpu.SemaphoreType.DMA
    scratch = [
        [half] * halves,
        [[[half] * halves for _ in range(n_row - 1)] for _ in range(2)],
        pltpu.VMEM((n_col, number, width, width), slots.dtype),
        pltpu.VMEM((8, 128), jnp.int32),
        pltpu.VMEM((n_col, 8, 128), jnp.int32),
        pltpu.SMEM((n_col, 8, 128), jnp.int32),
        pltpu.SMEM((groups * halves * number,), jnp.int32),
        pltpu.VMEM((n_col * number + 1, width, out_cols), jnp.float32),
        {
            "list_send": dma((n_col,)), "list_recv": dma((n_col,)),
            "slot_send": dma((n_col,)), "slot_recv": dma((n_col,)),
            "metric_send": dma((2, n_row - 1, halves)), "metric_recv": dma((2, n_row - 1, halves)),
            "own": dma((halves,)), "table": dma((1,)),
        },
    ]
    flat, tree = jax.tree.flatten(scratch)

    def body(list_ref, slots_ref, metric_ref, out_ref, *refs):
        kernel(n_row, n_col, list_ref, slots_ref, metric_ref, out_ref, *jax.tree.unflatten(tree, refs))

    return pl.pallas_call(
        body,
        out_shape=jax.ShapeDtypeStruct((PAIR_DEV, out_cols), jnp.float32),
        in_specs=[
            pl.BlockSpec(memory_space=pltpu.SMEM),
            pl.BlockSpec(memory_space=pl.ANY),
            pl.BlockSpec(memory_space=pl.ANY),
        ],
        out_specs=pl.BlockSpec(memory_space=pltpu.VMEM),
        scratch_shapes=flat,
        compiler_params=pltpu.CompilerParams(
            collective_id=0, has_side_effects=True, vmem_limit_bytes=40 * 1024 * 1024
        ),
    )(block_list, slots, metric.reshape(shard_blocks, width, out_cols))


def solution(mesh):
    return jax.shard_map(
        on_device,
        mesh=mesh,
        in_specs=(P(("row", "col"), None, None), P(("row", "col")), P("row", "col")),
        out_specs=P("row", "col"),
        check_vma=False,
    )
```

```python
import jax
import jax.numpy as jnp
from jax import lax
from jax.experimental import pallas as pl
from jax.experimental.pallas import tpu as pltpu
from jax.sharding import PartitionSpec as P

PAIR_DEV = 1024
MESH = pl.DeviceIdType.MESH


def kernel(n_row, n_col, list_ref, slots_ref, metric_ref, out_ref, own, held, packed, slots, few, own_list, lists, end_lists, table, end_table, prev, prod, sems):
    row, col = lax.axis_index("row"), lax.axis_index("col")
    number = list_ref.shape[0]
    pack = packed is not None
    halves = len(own)
    col_blocks, width = own[0].shape[0], own[0].shape[1]
    pair_blocks = out_ref.shape[0] // width
    zero = n_col * number

    def has(side, d):
        return row + d < n_row if side == 0 else row - d >= 0

    def toward(side):
        return row - 1 if side == 0 else row + 1

    def peer(d):
        return lax.rem(col + d, n_col)

    def end(side):
        return 0 if side == 0 else n_row - 1

    def gate(side):
        return 1 if side == 0 else n_row - 2

    def is_whole(d, h):
        return d == 0 and h == 0

    fetch = pltpu.make_async_copy(list_ref, few, sems["table"].at[0])
    fetch.start()

    barrier = pltpu.get_barrier_semaphore()
    for d in range(1, n_col):
        pl.semaphore_signal(barrier, inc=1, device_id=(row, peer(d)), device_id_type=MESH)
    for side in range(2):

        @pl.when(has(side, 1))
        def _():
            pl.semaphore_signal(barrier, inc=1, device_id=(toward(1 - side), col), device_id_type=MESH)

    expected = n_col - 1 + has(0, 1).astype(jnp.int32) + has(1, 1).astype(jnp.int32)
    if pack:
        for side in range(2):

            @pl.when(row == gate(side))
            def _():
                for d in range(1, n_col):
                    pl.semaphore_signal(barrier, inc=1, device_id=(end(side), peer(d)), device_id_type=MESH)

            expected += jnp.where(row == end(side), n_col - 1, 0)

    prod[zero] = jnp.zeros(prod.shape[1:], prod.dtype)
    fetch.wait()
    lane = lax.broadcasted_iota(jnp.int32, own_list.shape, 1)
    tile = jnp.full(own_list.shape, -1, jnp.int32)
    for s in range(number):
        tile = jnp.where(lane == s, few[s], tile)
    own_list[...] = tile
    pl.semaphore_wait(barrier, expected)

    def list_copy(d):
        return pltpu.make_async_remote_copy(
            src_ref=own_list, dst_ref=lists.at[col], send_sem=sems["list_send"].at[d], recv_sem=sems["list_recv"].at[d],
            device_id=(row, peer(d)), device_id_type=MESH,
        )

    def end_list_copy(side, d):
        return pltpu.make_async_remote_copy(
            src_ref=own_list, dst_ref=end_lists.at[col], send_sem=sems["end_send"].at[d], recv_sem=sems["end_recv"].at[d],
            device_id=(gate(side), peer(d)), device_id_type=MESH,
        )

    def slot_copy(d):
        return pltpu.make_async_remote_copy(
            src_ref=slots_ref, dst_ref=slots.at[col], send_sem=sems["slot_send"].at[d], recv_sem=sems["slot_recv"].at[d],
            device_id=(row, peer(d)), device_id_type=MESH,
        )

    def metric_copy(side, d, h):
        source = metric_ref.at[pl.ds(h * col_blocks, col_blocks)] if d == 0 else held[side][d - 1][h]
        return pltpu.make_async_remote_copy(
            src_ref=source, dst_ref=held[side][d][h],
            send_sem=sems["metric_send"].at[side, d, h], recv_sem=sems["metric_recv"].at[side, d, h],
            device_id=(toward(side), col), device_id_type=MESH,
        )

    def packed_copy(side, d, h):
        return pltpu.make_async_remote_copy(
            src_ref=packed[d][h], dst_ref=held[side][d][h].at[pl.ds(0, number)],
            send_sem=sems["metric_send"].at[side, d, h], recv_sem=sems["metric_recv"].at[side, d, h],
            device_id=(toward(side), col), device_id_type=MESH,
        )

    def for_metric(side, d, h, act, to_send):
        if not pack or is_whole(d, h):
            act(metric_copy(side, d, h))
            return
        at_end = row == (gate(side) if to_send else end(side))

        @pl.when(at_end)
        def _():
            act(packed_copy(side, d, h))

        @pl.when(jnp.logical_not(at_end))
        def _():
            act(metric_copy(side, d, h))

    def send(side, d, h):
        if pack and not is_whole(d, h):

            @pl.when(row == gate(side))
            def _():
                group = (row + d if side == 0 else row - d) * halves + h
                rows = own[h] if d == 0 else held[side][d - 1][h]
                for s in range(number):
                    v = jnp.maximum(end_table[group, 0, s], 0)
                    packed[d][h][s] = rows[lax.rem(v, jnp.int32(col_blocks))]

        for_metric(side, d, h, lambda copy: copy.start(), True)

    def own_copy(h):
        return pltpu.make_async_copy(metric_ref.at[pl.ds(h * col_blocks, col_blocks)], own[h], sems["own"].at[h])

    own_slots = pltpu.make_async_copy(slots_ref, slots.at[col], sems["slot_recv"].at[0])
    for d in range(1, n_col):
        list_copy(d).start()
    if pack:
        for side in range(2):

            @pl.when(row == end(side))
            def _():
                for d in range(n_col):
                    end_list_copy(side, d).start()

    for h in range(halves):
        for side in range(2):

            apart = not pack or is_whole(0, h)

            @pl.when(has(1 - side, 1) if apart else jnp.logical_and(has(1 - side, 1), row != gate(side)))
            def _():
                metric_copy(side, 0, h).start()

    for h in range(halves):
        own_copy(h).start()
    for d in range(1, n_col):
        slot_copy(d).start()
    own_slots.start()
    for h in range(halves):
        own_copy(h).wait()
    if pack:
        for side in range(2):

            @pl.when(row == gate(side))
            def _():
                for d in range(n_col):
                    end_list_copy(side, d).wait_recv()
                to_scalars = pltpu.make_async_copy(end_lists, end_table, sems["table"].at[1])
                to_scalars.start()
                to_scalars.wait()
                for h in range(1, halves):
                    send(side, 0, h)

    lists[col] = own_list[...]
    for d in range(1, n_col):
        list_copy(d).wait_recv()
    to_scalars = pltpu.make_async_copy(lists, table, sems["table"].at[0])
    to_scalars.start()
    to_scalars.wait()

    steps = [(0, 0)] + [(side, d) for d in range(1, n_row) for side in range(2)]
    last = [jnp.int32(zero)] * pair_blocks
    for at, (side, d) in enumerate(steps):
        shard = row + d if side == 0 else row - d
        valid = has(side, d)
        shard = jnp.clip(shard, 0, n_row - 1)
        for h in range(halves):
            group = shard * halves + h
            for s in range(number):
                v = table[group, 0, s]
                pair = jnp.where(jnp.logical_and(valid, v >= 0), lax.div(jnp.maximum(v, 0), jnp.int32(col_blocks)), -1)
                before = jnp.int32(zero)
                here = group * number + s
                for p in range(pair_blocks):
                    before = jnp.where(pair == p, last[p], before)
                    last[p] = jnp.where(pair == p, here, last[p])
                prev[(at * halves + h) * number + s] = before

    def forward(d):
        for h in range(halves):
            for side in range(2):

                @pl.when(has(side, d))
                def _():
                    for_metric(side, d - 1, h, lambda copy: copy.wait_recv(), False)
                    if d < n_row - 1:

                        @pl.when(has(1 - side, 1))
                        def _():
                            send(side, d, h)

    def compute(at):
        side, d = steps[at]
        shard = row + d if side == 0 else row - d

        @pl.when(has(side, d))
        def _():
            for h in range(halves):
                group = shard * halves + h
                rows = own[h] if d == 0 else held[side][d - 1][h]
                arrived = sems["slot_recv"].at[lax.rem(col - group + n_col, n_col)]
                pltpu.make_async_copy(slots_ref, slots.at[group], arrived).wait()
                for s in range(number):
                    v = jnp.maximum(table[group, 0, s], 0)
                    before = prev[(at * halves + h) * number + s]
                    at_block = lax.rem(v, jnp.int32(col_blocks))
                    if pack and d > 0 and not is_whole(d - 1, h):
                        at_block = jnp.where(row == end(side), s, at_block)
                    block = rows[at_block]
                    product = jnp.dot(slots[group, s], block, preferred_element_type=jnp.float32)
                    prod[group * number + s] = prod[before] + product

    forward(1)
    compute(0)
    for d in range(1, n_row):
        if d < n_row - 1:
            forward(d + 1)
        compute(2 * d - 1)
        compute(2 * d)

    for p in range(pair_blocks):
        out_ref[pl.ds(p * width, width)] = prod[last[p]]

    for d in range(1, n_col):
        list_copy(d).wait_send()
        slot_copy(d).wait_send()
    for d in range(n_row - 1):
        for h in range(halves):
            for side in range(2):

                @pl.when(jnp.logical_and(has(side, d), has(1 - side, 1)))
                def _():
                    for_metric(side, d, h, lambda copy: copy.wait_send(), True)

    if pack:
        for side in range(2):

            @pl.when(row == end(side))
            def _():
                for d in range(n_col):
                    end_list_copy(side, d).wait_send()


def on_device(slots, block_list, metric):
    n_row, n_col = lax.axis_size("row"), lax.axis_size("col")
    number, width = slots.shape[:2]
    out_cols = metric.shape[1]
    halves = n_col // n_row
    shard_blocks = metric.shape[0] // width
    col_blocks = shard_blocks // halves
    half = pltpu.VMEM((col_blocks, width, out_cols), metric.dtype)
    groups = 2 * n_row - 1
    pack = n_row >= 4 and number < col_blocks
    few = pltpu.VMEM((number, width, out_cols), metric.dtype)
    dma = pltpu.SemaphoreType.DMA
    scratch = [
        [half] * halves,
        [[[half] * halves for _ in range(n_row - 1)] for _ in range(2)],
        [[few] * halves for _ in range(n_row - 1)] if pack else None,
        pltpu.VMEM((n_col, number, width, width), slots.dtype),
        pltpu.SMEM((number,), jnp.int32),
        pltpu.VMEM((8, 128), jnp.int32),
        pltpu.VMEM((n_col, 8, 128), jnp.int32),
        pltpu.VMEM((n_col, 8, 128), jnp.int32),
        pltpu.SMEM((n_col, 8, 128), jnp.int32),
        pltpu.SMEM((n_col, 8, 128), jnp.int32),
        pltpu.SMEM((groups * halves * number,), jnp.int32),
        pltpu.VMEM((n_col * number + 1, width, out_cols), jnp.float32),
        {
            "list_send": dma((n_col,)), "list_recv": dma((n_col,)),
            "slot_send": dma((n_col,)), "slot_recv": dma((n_col,)),
            "metric_send": dma((2, n_row - 1, halves)), "metric_recv": dma((2, n_row - 1, halves)),
            "own": dma((halves,)), "table": dma((2,)), "end_send": dma((n_col,)), "end_recv": dma((n_col,)),
        },
    ]
    flat, tree = jax.tree.flatten(scratch)

    def body(list_ref, slots_ref, metric_ref, out_ref, *refs):
        kernel(n_row, n_col, list_ref, slots_ref, metric_ref, out_ref, *jax.tree.unflatten(tree, refs))

    return pl.pallas_call(
        body,
        out_shape=jax.ShapeDtypeStruct((PAIR_DEV, out_cols), jnp.float32),
        in_specs=[
            pl.BlockSpec(memory_space=pltpu.HBM),
            pl.BlockSpec(memory_space=pltpu.HBM),
            pl.BlockSpec(memory_space=pltpu.HBM),
        ],
        out_specs=pl.BlockSpec(memory_space=pltpu.VMEM),
        scratch_shapes=flat,
        compiler_params=pltpu.CompilerParams(
            collective_id=0, has_side_effects=True, vmem_limit_bytes=40 * 1024 * 1024
        ),
    )(block_list, slots, metric.reshape(shard_blocks, width, out_cols))


def solution(mesh):
    return jax.shard_map(
        on_device,
        mesh=mesh,
        in_specs=(P(("row", "col"), None, None), P(("row", "col")), P("row", "col")),
        out_specs=P("row", "col"),
        check_vma=False,
    )
```

```python
import jax
import jax.numpy as jnp
from jax import lax
from jax.experimental import pallas as pl
from jax.experimental.pallas import tpu as pltpu
from jax.sharding import PartitionSpec as P

PAIR_DEV = 1024
MESH = pl.DeviceIdType.MESH


def kernel(n_row, n_col, list_ref, slots_ref, metric_ref, out_ref, own, held, packed, slots, few, own_list, lists, end_lists, table, end_table, prev, prod, sems):
    row, col = lax.axis_index("row"), lax.axis_index("col")
    number = list_ref.shape[0]
    pack = packed is not None
    halves = len(own)
    col_blocks, width = own[0].shape[0], own[0].shape[1]
    pair_blocks = out_ref.shape[0] // width
    zero = n_col * number

    def has(side, d):
        return row + d < n_row if side == 0 else row - d >= 0

    def toward(side):
        return row - 1 if side == 0 else row + 1

    def peer(d):
        return lax.rem(col + d, n_col)

    def end(side):
        return 0 if side == 0 else n_row - 1

    def gate(side):
        return 1 if side == 0 else n_row - 2

    def is_whole(d, h):
        return d == 0 and h == 0

    fetch = pltpu.make_async_copy(list_ref, few, sems["table"].at[0])
    fetch.start()

    barrier = pltpu.get_barrier_semaphore()
    for d in range(1, n_col):
        pl.semaphore_signal(barrier, inc=1, device_id=(row, peer(d)), device_id_type=MESH)
    for side in range(2):

        @pl.when(has(side, 1))
        def _():
            pl.semaphore_signal(barrier, inc=1, device_id=(toward(1 - side), col), device_id_type=MESH)

    expected = n_col - 1 + has(0, 1).astype(jnp.int32) + has(1, 1).astype(jnp.int32)
    if pack:
        for side in range(2):

            @pl.when(row == gate(side))
            def _():
                for d in range(1, n_col):
                    pl.semaphore_signal(barrier, inc=1, device_id=(end(side), peer(d)), device_id_type=MESH)

            expected += jnp.where(row == end(side), n_col - 1, 0)

    prod[zero] = jnp.zeros(prod.shape[1:], prod.dtype)
    fetch.wait()
    lane = lax.broadcasted_iota(jnp.int32, own_list.shape, 1)
    tile = jnp.full(own_list.shape, -1, jnp.int32)
    for s in range(number):
        tile = jnp.where(lane == s, few[s], tile)
    own_list[...] = tile
    pl.semaphore_wait(barrier, expected)

    def list_copy(d):
        return pltpu.make_async_remote_copy(
            src_ref=own_list, dst_ref=lists.at[col], send_sem=sems["list_send"].at[d], recv_sem=sems["list_recv"].at[d],
            device_id=(row, peer(d)), device_id_type=MESH,
        )

    sibling = col + 1 - 2 * lax.rem(col, 2)

    def relay_copy(e):
        source = lax.rem(col - e + n_col, n_col)
        return pltpu.make_async_remote_copy(
            src_ref=slots_ref if e == 0 else slots.at[source], dst_ref=slots.at[source],
            send_sem=sems["slot_send"].at[e + 1], recv_sem=sems["slot_recv"].at[e + 1],
            device_id=(row, sibling), device_id_type=MESH,
        )

    def end_list_copy(side, d):
        return pltpu.make_async_remote_copy(
            src_ref=own_list, dst_ref=end_lists.at[col], send_sem=sems["end_send"].at[d], recv_sem=sems["end_recv"].at[d],
            device_id=(gate(side), peer(d)), device_id_type=MESH,
        )

    def slot_copy(d):
        return pltpu.make_async_remote_copy(
            src_ref=slots_ref, dst_ref=slots.at[col], send_sem=sems["slot_send"].at[d], recv_sem=sems["slot_recv"].at[d],
            device_id=(row, peer(d)), device_id_type=MESH,
        )

    def metric_copy(side, d, h):
        source = metric_ref.at[pl.ds(h * col_blocks, col_blocks)] if d == 0 else held[side][d - 1][h]
        return pltpu.make_async_remote_copy(
            src_ref=source, dst_ref=held[side][d][h],
            send_sem=sems["metric_send"].at[side, d, h], recv_sem=sems["metric_recv"].at[side, d, h],
            device_id=(toward(side), col), device_id_type=MESH,
        )

    def packed_copy(side, d, h):
        return pltpu.make_async_remote_copy(
            src_ref=packed[d][h], dst_ref=held[side][d][h].at[pl.ds(0, number)],
            send_sem=sems["metric_send"].at[side, d, h], recv_sem=sems["metric_recv"].at[side, d, h],
            device_id=(toward(side), col), device_id_type=MESH,
        )

    def for_metric(side, d, h, act, to_send):
        if not pack or is_whole(d, h):
            act(metric_copy(side, d, h))
            return
        at_end = row == (gate(side) if to_send else end(side))

        @pl.when(at_end)
        def _():
            act(packed_copy(side, d, h))

        @pl.when(jnp.logical_not(at_end))
        def _():
            act(metric_copy(side, d, h))

    def send(side, d, h):
        if pack and not is_whole(d, h):

            @pl.when(row == gate(side))
            def _():
                group = (row + d if side == 0 else row - d) * halves + h
                rows = own[h] if d == 0 else held[side][d - 1][h]
                for s in range(number):
                    v = jnp.maximum(end_table[group, 0, s], 0)
                    packed[d][h][s] = rows[lax.rem(v, jnp.int32(col_blocks))]

        for_metric(side, d, h, lambda copy: copy.start(), True)

    def own_copy(h):
        return pltpu.make_async_copy(metric_ref.at[pl.ds(h * col_blocks, col_blocks)], own[h], sems["own"].at[h])

    own_slots = pltpu.make_async_copy(slots_ref, slots.at[col], sems["slot_recv"].at[0])
    for d in range(1, n_col):
        list_copy(d).start()
    if pack:
        for side in range(2):

            @pl.when(row == end(side))
            def _():
                for d in range(n_col):
                    end_list_copy(side, d).start()

    for h in range(halves):
        for side in range(2):

            apart = not pack or is_whole(0, h)

            @pl.when(has(1 - side, 1) if apart else jnp.logical_and(has(1 - side, 1), row != gate(side)))
            def _():
                metric_copy(side, 0, h).start()

    for h in range(halves):
        own_copy(h).start()
    for d in range(2, n_col, 2):
        slot_copy(d).start()
    relay_copy(0).start()
    own_slots.start()
    for h in range(halves):
        own_copy(h).wait()
    if pack:
        for side in range(2):

            @pl.when(row == gate(side))
            def _():
                for d in range(n_col):
                    end_list_copy(side, d).wait_recv()
                to_scalars = pltpu.make_async_copy(end_lists, end_table, sems["table"].at[1])
                to_scalars.start()
                to_scalars.wait()
                for h in range(1, halves):
                    send(side, 0, h)

    lists[col] = own_list[...]
    for d in range(1, n_col):
        list_copy(d).wait_recv()
    to_scalars = pltpu.make_async_copy(lists, table, sems["table"].at[0])
    to_scalars.start()
    to_scalars.wait()

    steps = [(0, 0)] + [(side, d) for d in range(1, n_row) for side in range(2)]
    last = [jnp.int32(zero)] * pair_blocks
    turns = [(at, h) for d in range(n_row) for h in range(halves) for at in range(len(steps)) if steps[at][1] == d]
    for at, h in turns:
        side, d = steps[at]
        valid = has(side, d)
        shard = jnp.clip(row + d if side == 0 else row - d, 0, n_row - 1)
        group = shard * halves + h
        for s in range(number):
            v = table[group, 0, s]
            pair = jnp.where(jnp.logical_and(valid, v >= 0), lax.div(jnp.maximum(v, 0), jnp.int32(col_blocks)), -1)
            before = jnp.int32(zero)
            here = group * number + s
            for p in range(pair_blocks):
                before = jnp.where(pair == p, last[p], before)
                last[p] = jnp.where(pair == p, here, last[p])
            prev[(at * halves + h) * number + s] = before

    def forward(d, h):
        for side in range(2):

            @pl.when(has(side, d))
            def _():
                for_metric(side, d - 1, h, lambda copy: copy.wait_recv(), False)
                if d < n_row - 1:

                    @pl.when(has(1 - side, 1))
                    def _():
                        send(side, d, h)

    def relay():
        own_slots.wait()
        for e in range(2, n_col, 2):
            slot_copy(e).wait_recv()
            relay_copy(e).start()

    def compute(d, h):
        for at, (side, distance) in enumerate(steps):
            if distance == d:
                compute_side(at, side, d, h)

    def compute_side(at, side, d, h):
        shard = row + d if side == 0 else row - d

        @pl.when(has(side, d))
        def _():
            group = shard * halves + h
            rows = own[h] if d == 0 else held[side][d - 1][h]

            @pl.when(lax.rem(group + col, 2) == 1)
            def _():
                arrived = sems["slot_recv"].at[lax.rem(sibling - group + n_col, n_col) + 1]
                pltpu.make_async_copy(slots_ref, slots.at[group], arrived).wait()

            for s in range(number):
                v = jnp.maximum(table[group, 0, s], 0)
                before = prev[(at * halves + h) * number + s]
                at_block = lax.rem(v, jnp.int32(col_blocks))
                if pack and d > 0 and not is_whole(d - 1, h):
                    at_block = jnp.where(row == end(side), s, at_block)
                product = jnp.dot(slots[group, s], rows[at_block], preferred_element_type=jnp.float32)
                prod[group * number + s] = prod[before] + product

    for h in range(halves):
        forward(1, h)
    relay()
    for d in range(2):
        for h in range(halves):
            compute(d, h)
    for d in range(2, n_row):
        for h in range(halves):
            forward(d, h)
            compute(d, h)

    for p in range(pair_blocks):
        out_ref[pl.ds(p * width, width)] = prod[last[p]]

    for d in range(1, n_col):
        list_copy(d).wait_send()
    for d in range(0, n_col, 2):
        if d > 0:
            slot_copy(d).wait_send()
        relay_copy(d).wait_send()
    for d in range(n_row - 1):
        for h in range(halves):
            for side in range(2):

                @pl.when(jnp.logical_and(has(side, d), has(1 - side, 1)))
                def _():
                    for_metric(side, d, h, lambda copy: copy.wait_send(), True)

    if pack:
        for side in range(2):

            @pl.when(row == end(side))
            def _():
                for d in range(n_col):
                    end_list_copy(side, d).wait_send()


def on_device(slots, block_list, metric):
    n_row, n_col = lax.axis_size("row"), lax.axis_size("col")
    number, width = slots.shape[:2]
    out_cols = metric.shape[1]
    halves = n_col // n_row
    shard_blocks = metric.shape[0] // width
    col_blocks = shard_blocks // halves
    half = pltpu.VMEM((col_blocks, width, out_cols), metric.dtype)
    groups = 2 * n_row - 1
    pack = n_row >= 4 and number < col_blocks
    few = pltpu.VMEM((number, width, out_cols), metric.dtype)
    dma = pltpu.SemaphoreType.DMA
    scratch = [
        [half] * halves,
        [[[half] * halves for _ in range(n_row - 1)] for _ in range(2)],
        [[few] * halves for _ in range(n_row - 1)] if pack else None,
        pltpu.VMEM((n_col, number, width, width), slots.dtype),
        pltpu.SMEM((number,), jnp.int32),
        pltpu.VMEM((8, 128), jnp.int32),
        pltpu.VMEM((n_col, 8, 128), jnp.int32),
        pltpu.VMEM((n_col, 8, 128), jnp.int32),
        pltpu.SMEM((n_col, 8, 128), jnp.int32),
        pltpu.SMEM((n_col, 8, 128), jnp.int32),
        pltpu.SMEM((groups * halves * number,), jnp.int32),
        pltpu.VMEM((n_col * number + 1, width, out_cols), jnp.float32),
        {
            "list_send": dma((n_col,)), "list_recv": dma((n_col,)),
            "slot_send": dma((n_col,)), "slot_recv": dma((n_col,)),
            "metric_send": dma((2, n_row - 1, halves)), "metric_recv": dma((2, n_row - 1, halves)),
            "own": dma((halves,)), "table": dma((2,)), "end_send": dma((n_col,)), "end_recv": dma((n_col,)),
        },
    ]
    flat, tree = jax.tree.flatten(scratch)

    def body(list_ref, slots_ref, metric_ref, out_ref, *refs):
        kernel(n_row, n_col, list_ref, slots_ref, metric_ref, out_ref, *jax.tree.unflatten(tree, refs))

    return pl.pallas_call(
        body,
        out_shape=jax.ShapeDtypeStruct((PAIR_DEV, out_cols), jnp.float32),
        in_specs=[
            pl.BlockSpec(memory_space=pltpu.HBM),
            pl.BlockSpec(memory_space=pltpu.HBM),
            pl.BlockSpec(memory_space=pltpu.HBM),
        ],
        out_specs=pl.BlockSpec(memory_space=pltpu.VMEM),
        scratch_shapes=flat,
        compiler_params=pltpu.CompilerParams(
            collective_id=0, has_side_effects=True, vmem_limit_bytes=56 * 1024 * 1024
        ),
    )(block_list, slots, metric.reshape(shard_blocks, width, out_cols))


def solution(mesh):
    return jax.shard_map(
        on_device,
        mesh=mesh,
        in_specs=(P(("row", "col"), None, None), P(("row", "col")), P("row", "col")),
        out_specs=P("row", "col"),
        check_vma=False,
    )
```
